128 devices in a mesh: row: 8 (over y, core), col: 16 (over z, x).
Axes of the slice: x: 4, y: 4, z: 4, core: 2. Of those that a mesh axis runs over, the one named last changes fastest.
Arguments:
- theta: bfloat16 [6144, 6144], P('row', 'col'), may hold values from -8 to 8
- start_basis: bfloat16 [6144, 2048], P('row', 'col'), may hold values from -6 to 6
Outputs:
- subspace: bfloat16 [6144, 2048], P('row', 'col')
- gram: float32 [2048, 2048], P('col', 'row')
The draws below stay inside these ranges and needn't reach their ends.
All inputs are finite; a program needn't handle non-finite values.
Results may differ from the reference program's by a relative error of at most 0.0042.
Values may be sent and summed in bfloat16 or wider, within the bound.
No kernel may reach another device: no remote copies, remote signals or barrier semaphores. Data moves between devices by JAX's collectives and lax.ppermute only.
A program may use at most 128 MiB of HBM per device.

```python
import jax
import jax.numpy as jnp

ORDER = 6144
SUBSPACE = 2048


def draw_theta(key, part):
    keys = jax.random.split(jax.random.fold_in(key, 11), 3)
    index = jnp.arange(ORDER).astype(jnp.float32)
    rising = jnp.sqrt(1.0 + 2.0 * index / ORDER)
    row_scale = jnp.exp(jax.random.uniform(keys[0], (ORDER,), jnp.float32, -0.2, 0.2)) * rising
    col_scale = jnp.exp(jax.random.uniform(keys[1], (ORDER,), jnp.float32, -1.15, 1.15)) * rising
    base = jnp.clip(jax.random.normal(keys[2], (ORDER, ORDER), jnp.float32), -6.0, 6.0)
    values = base * row_scale[:, None] * col_scale[None, :] / jnp.sqrt(jnp.float32(ORDER))
    return values.astype(jnp.bfloat16)


def shard_levels(stream_key, shape, pieces, low, top_value):
    gain, own = 1.0, jax.random.fold_in(stream_key, 6)
    for position, blocks in pieces:
        draws = jnp.exp(jax.random.uniform(jax.random.fold_in(own, position), (blocks,), jnp.float32, low / len(pieces), top_value / len(pieces)))
        gain = gain * jnp.repeat(draws, shape[position] // blocks).reshape([-1 if axis == position else 1 for axis in range(len(shape))])
    return gain


def normal_values(key, shape, width, most, cuts=(), dtype=jnp.bfloat16):
    level = shard_levels(key, shape, cuts, -0.22, 0.18) if cuts else 1.0
    entries = jax.random.normal(key, shape, jnp.float32) * width * level
    return jnp.minimum(jnp.maximum(entries, -most), most).astype(dtype)


def setup_inputs(seed: int = 0) -> dict:
    splits = jax.random.split(jax.random.key(seed), 3)
    return {
        "theta": draw_theta(jax.random.fold_in(splits[2], 71), 0),
        "start_basis": normal_values(splits[1], (ORDER, SUBSPACE), 1.0, 6.0, ((0, 8), (1, 16))),
    }


def reference(theta, start_basis):
    fro = jnp.sum(theta.astype(jnp.float32) ** 2)
    raw = jnp.dot(theta, theta.T, preferred_element_type=jnp.float32)
    density = (raw * (ORDER / (4.0 * fro))).astype(jnp.bfloat16)
    first = jnp.dot(density, start_basis, preferred_element_type=jnp.float32).astype(jnp.bfloat16)
    subspace = jnp.dot(density, first, preferred_element_type=jnp.float32).astype(jnp.bfloat16)
    gram = jnp.dot(subspace.T, subspace, preferred_element_type=jnp.float32) / ORDER
    return subspace, gram
```

```python
import jax
import jax.numpy as jnp
from jax import lax
from jax.sharding import Mesh, PartitionSpec as P

ORDER = 6144
ALL = ("y", "core", "z", "x")


def other_core(x):
    return lax.ppermute(x, "core", [(0, 1), (1, 0)])


def core_sum_half(parts, core):
    mine = lax.dynamic_index_in_dim(parts, core, 0, keepdims=False)
    theirs = lax.dynamic_index_in_dim(parts, 1 - core, 0, keepdims=False)
    return mine + other_core(theirs)


def three_terms(value, width):
    high = lax.reduce_precision(value, 8, 7)
    mid = lax.reduce_precision(value - high, 8, 7)
    low = value - high - mid
    rows = jnp.stack([high, mid, low] + [jnp.zeros_like(value)] * 13)
    return jnp.broadcast_to(rows[:, None], (16, width)).astype(jnp.bfloat16)


def sum_over_rows(part, core, square=None):
    n, width = part.shape
    half = core_sum_half(part.reshape(2, n // 2, width), core)
    pieces = half.astype(jnp.bfloat16).reshape(4, n // 8, width)
    if square is not None:
        square = square + other_core(jnp.full((8, 128), square))[0, 0]
        extra = jnp.broadcast_to(three_terms(square, width)[None], (4, 16, width))
        pieces = jnp.concatenate([pieces, extra], 1)
    got = lax.all_to_all(pieces, "y", 0, 0).astype(jnp.float32)
    total = jnp.sum(got[:, n // 8 :, 0])
    piece = jnp.sum(got[:, : n // 8], axis=0).astype(jnp.bfloat16)
    mine = lax.all_gather(piece, "y", axis=0).reshape(n // 2, width)
    theirs = other_core(mine)
    first = core == 0
    return jnp.concatenate([jnp.where(first, mine, theirs), jnp.where(first, theirs, mine)], 0), total


def per_device(theta, basis):
    core = lax.axis_index("core")
    slab = lax.all_gather(theta, ("z", "x"), axis=0)
    square = jnp.sum(slab.astype(jnp.float32) ** 2)

    def down(x, square=None):
        out = lax.dot_general(slab, x, (((1,), (0,)), ((), ())), preferred_element_type=jnp.float32)
        return sum_over_rows(out.reshape(-1, x.shape[1]), core, square)

    def up(t, scale):
        t = t.reshape(slab.shape[0], slab.shape[2], -1)
        out = lax.dot_general(slab, t, (((0, 2), (0, 1)), ((), ())), preferred_element_type=jnp.float32)
        return (out * scale).astype(jnp.bfloat16)

    total, fro = down(basis, square)
    scale = ORDER / (4.0 * fro)
    first = up(total, scale)
    subspace = up(down(first)[0], scale)

    along_x = lax.all_gather(subspace, "x", axis=0)
    along_z = lax.all_gather(subspace, "z", axis=0)
    part = jnp.einsum("brn,arm->bamn", along_z, along_x, preferred_element_type=jnp.float32)
    part = part.reshape(4, 4, 2, 64, 128).transpose(2, 0, 1, 3, 4).reshape(2, 16, 64, 128)
    half = core_sum_half(part, core)
    got = lax.all_to_all(half, ("y", "x"), 0, 0).reshape(4, 4, 64, 128)
    rows = jnp.sum(got, axis=0).reshape(2, 2, 64, 128)
    mine = lax.dynamic_index_in_dim(rows, core, 0, keepdims=False)
    theirs = other_core(lax.dynamic_index_in_dim(rows, 1 - core, 0, keepdims=False))
    first_half = core == 0
    both = jnp.stack([jnp.where(first_half, mine, theirs), jnp.where(first_half, theirs, mine)])
    gram = both.transpose(0, 2, 1, 3).reshape(128, 256) / ORDER
    return subspace, gram


def solution(mesh):
    sizes = (mesh.shape["row"] // 2, 2, 4, mesh.shape["col"] // 4)
    fine = Mesh(mesh.devices.reshape(sizes), ALL)
    spec = P(("y", "core"), ("z", "x"))
    return jax.shard_map(
        per_device,
        mesh=fine,
        in_specs=(spec, spec),
        out_specs=(spec, P(("z", "x"), ("y", "core"))),
        check_vma=False,
    )
```

```python
import jax
import jax.numpy as jnp
from jax import lax
from jax.experimental import pallas as pl
from jax.experimental.pallas import tpu as pltpu
from jax.sharding import Mesh, PartitionSpec as P

ORDER = 6144
ALL = ("y", "core", "z", "x")
COLS = 384
BLOCKS = 16


def shift(x, axis, by):
    return lax.ppermute(x, axis, [(i, (i + by) % 4) for i in range(4)])


def other_core(x):
    return lax.ppermute(x, "core", [(0, 1), (1, 0)])


def f32_dot(left, right, dims):
    return lax.dot_general(left, right, (dims, ((), ())), preferred_element_type=jnp.float32)


def gather_plane(own):
    rows = own.shape[0]
    half, quarter = rows // 2, rows // 4
    xp, xm, zp, zm = lax.optimization_barrier(
        (shift(own, "x", 1), shift(own, "x", 3), shift(own, "z", 1), shift(own, "z", 3))
    )
    a, b, c, d = lax.optimization_barrier(
        (
            shift(jnp.concatenate([zp, xp[:half]]), "x", 1),
            shift(jnp.concatenate([zm, xm[half:]]), "x", 3),
            shift(jnp.concatenate([xm, zp[:half]]), "z", 1),
            shift(jnp.concatenate([xp, zm[half:]]), "z", 3),
        )
    )
    far_x = jnp.concatenate([a[rows:], b[rows:]])
    far_z = jnp.concatenate([c[rows:], d[rows:]])
    e, f, g, h = lax.optimization_barrier(
        (shift(far_z, "x", 1), shift(far_z, "x", 3), shift(far_x, "z", 1), shift(far_x, "z", 3))
    )
    last = jnp.concatenate(
        lax.optimization_barrier(
            (
                shift(e[:quarter], "x", 1),
                shift(f[quarter:half], "x", 3),
                shift(g[half : half + quarter], "z", 1),
                shift(h[half + quarter :], "z", 3),
            )
        )
    )
    return [own, xp, xm, zp, zm], [a, b, c, d, far_x, far_z], [e, f, g, h], [last]


def three_terms(value):
    high = lax.reduce_precision(value, 8, 7)
    mid = lax.reduce_precision(value - high, 8, 7)
    low = value - high - mid
    lane = lax.broadcasted_iota(jnp.int32, (16, 128), 1)
    row = lax.broadcasted_iota(jnp.int32, (16, 128), 0)
    terms = jnp.where(lane == 0, high, jnp.where(lane == 1, mid, jnp.where(lane == 2, low, 0.0)))
    return jnp.where(row == 0, terms, 0.0).astype(jnp.bfloat16)


def sum_over_rows(mine, theirs, square=None):
    n = mine.shape[1]
    half = mine + other_core(theirs)
    send = half.astype(jnp.bfloat16)
    if square is not None:
        square = square + other_core(jnp.full((8, 128), square))[0, 0]
        extra = jnp.tile(three_terms(square), (4, 1))
        send = jnp.concatenate([send, extra], 1)
    got = [shift(send[16 * d : 16 * d + 16], "y", d) for d in (1, 3, 2)]
    total = half[:16]
    for piece in got:
        total = total + piece[:, :n].astype(jnp.float32)
    fro = None
    if square is not None:
        fro = square + sum(jnp.sum(piece[:, n:].astype(jnp.float32)) for piece in got)
    piece = total.astype(jnp.bfloat16)
    up1, up3, up2 = (shift(piece, "y", 4 - d) for d in (1, 3, 2))
    whole = jnp.concatenate([piece, up1, up2, up3])
    return jnp.concatenate([whole, other_core(whole)]), fro


def apply_kernel(down, scale_ref, t_ref, *refs):
    theta_refs = refs[:BLOCKS]
    outs = refs[BLOCKS : BLOCKS + (2 if down else 1)]
    theta, sems = refs[-2:]
    rows = theta.shape[1]
    copies = []
    for i, ref in enumerate(theta_refs):
        copy = pltpu.make_async_copy(ref.at[pl.ds(0, rows)], theta.at[i], sems.at[i])
        copy.start()
        copies.append(copy)
    total = jnp.zeros((t_ref.shape[0], rows), jnp.float32)
    for i, copy in enumerate(copies):
        copy.wait()
        total += f32_dot(t_ref[:, i * COLS : (i + 1) * COLS], theta[i], ((1,), (1,)))
    x = (total * scale_ref[0, 0]).astype(jnp.bfloat16)
    if not down:
        outs[0][...] = x
        return
    for i in range(BLOCKS):
        part = f32_dot(x, theta[i], ((1,), (0,)))
        outs[0][:, i * COLS : (i + 1) * COLS] = part[:64]
        outs[1][:, i * COLS : (i + 1) * COLS] = part[64:]


def apply(scale, t, blocks, down):
    width, n = t.shape
    rows = blocks[0].shape[0]
    if down:
        out_shape = [jax.ShapeDtypeStruct((64, n), jnp.float32)] * 2
    else:
        out_shape = [jax.ShapeDtypeStruct((width, rows), jnp.bfloat16)]
    vmem = pl.BlockSpec(memory_space=pltpu.VMEM)
    return pl.pallas_call(
        lambda *refs: apply_kernel(down, *refs),
        out_shape=out_shape,
        in_specs=[pl.BlockSpec(memory_space=pltpu.SMEM), vmem] + [pl.BlockSpec(memory_space=pl.ANY)] * BLOCKS,
        out_specs=[vmem] * len(out_shape),
        scratch_shapes=[
            pltpu.VMEM((BLOCKS, rows, COLS), jnp.bfloat16),
            pltpu.SemaphoreType.DMA((BLOCKS,)),
        ],
        compiler_params=pltpu.CompilerParams(vmem_limit_bytes=32 * 2**20),
        cost_estimate=pl.CostEstimate(
            flops=(4 if down else 2) * width * n * rows, bytes_accessed=2 * n * rows, transcendentals=0
        ),
    )(scale.reshape(1, 1), t, *blocks)


def column_order(y, core):
    place = lax.broadcasted_iota(jnp.int32, (128, 128), 0)
    column = lax.broadcasted_iota(jnp.int32, (128, 128), 1)
    half = (place // 64 + core) % 2
    group = (place // 16 + y) % 4
    return (column == half * 64 + group * 16 + place % 16).astype(jnp.bfloat16)


def per_device(theta, basis):
    core, y = lax.axis_index("core"), lax.axis_index("y")
    order = column_order(y, core)
    x = f32_dot(order, basis, ((1,), (1,))).astype(jnp.bfloat16)

    blocks, parts, square = [], [], 0.0
    rows = theta.shape[0]
    for step in gather_plane(theta):
        for block in step:
            block_rows = block[:rows]
            parts.append(f32_dot(x, block_rows, ((1,), (0,))))
            square = square + jnp.sum(block_rows.astype(jnp.float32) ** 2)
            blocks.append(block)
    mine = jnp.concatenate([p[:64] for p in parts], 1)
    theirs = jnp.concatenate([p[64:] for p in parts], 1)
    t, fro = sum_over_rows(mine, theirs, square)
    scale = ORDER / (4.0 * fro)
    t, _ = sum_over_rows(*apply(scale, t, blocks, True))
    (x,) = apply(scale, t, blocks, False)
    subspace = f32_dot(x, order, ((0,), (0,))).astype(jnp.bfloat16)

    along_x = lax.all_gather(subspace, "x", axis=0)
    along_z = lax.all_to_all(jnp.broadcast_to(subspace[None], (4, *subspace.shape)), "z", 0, 0)
    part = jnp.einsum("brn,arm->bamn", along_z, along_x, preferred_element_type=jnp.float32)
    part = part.reshape(4, 4, 2, 64, 128).transpose(2, 0, 1, 3, 4).reshape(2, 16, 64, 128)
    keep = lax.dynamic_index_in_dim(part, core, 0, keepdims=False)
    half = keep + other_core(lax.dynamic_index_in_dim(part, 1 - core, 0, keepdims=False))
    got = lax.all_to_all(half, ("y", "x"), 0, 0).reshape(4, 4, 64, 128)
    sums = jnp.sum(got, axis=0).reshape(2, 2, 64, 128)
    keep = lax.dynamic_index_in_dim(sums, core, 0, keepdims=False)
    theirs = other_core(lax.dynamic_index_in_dim(sums, 1 - core, 0, keepdims=False))
    first_half = core == 0
    both = jnp.stack([jnp.where(first_half, keep, theirs), jnp.where(first_half, theirs, keep)])
    gram = both.transpose(0, 2, 1, 3).reshape(128, 256) / ORDER
    return subspace, gram


def solution(mesh):
    fine = Mesh(mesh.devices.reshape(4, 2, 4, 4), ALL)
    spec = P(("y", "core"), ("z", "x"))
    return jax.shard_map(
        per_device,
        mesh=fine,
        in_specs=(spec, spec),
        out_specs=(spec, P(("z", "x"), ("y", "core"))),
        check_vma=False,
    )
```

```python
import jax
import jax.numpy as jnp
from jax import lax
from jax.experimental import pallas as pl
from jax.experimental.pallas import tpu as pltpu
from jax.sharding import Mesh, PartitionSpec as P

ORDER = 6144
ALL = ("y", "core", "z", "x")
COLS = 384
BLOCKS = 16


def shift(x, axis, by):
    return lax.ppermute(x, axis, [(i, (i + by) % 4) for i in range(4)])


def other_core(x):
    return lax.ppermute(x, "core", [(0, 1), (1, 0)])


def f32_dot(left, right, dims):
    return lax.dot_general(left, right, (dims, ((), ())), preferred_element_type=jnp.float32)


def gather_plane(own):
    half = own.shape[0] // 2
    xp, xm, zp, zm = lax.optimization_barrier(
        (shift(own, "x", 1), shift(own, "x", 3), shift(own, "z", 1), shift(own, "z", 3))
    )
    pp, mm, pm, mp = lax.optimization_barrier(
        (shift(zp, "x", 1), shift(zm, "x", 3), shift(xm, "z", 1), shift(xp, "z", 3))
    )
    a, b, c, d = lax.optimization_barrier(
        (shift(mp, "x", 1), shift(pm, "x", 3), shift(pp, "z", 1), shift(mm, "z", 3))
    )
    far_x, far_z, low, high = lax.optimization_barrier(
        (shift(xp, "x", 1), shift(zp, "z", 1), shift(d[:half], "x", 3), shift(a[half:], "z", 3))
    )
    return [own, xp, xm, zp, zm], [pp, mm, pm, mp], [a, b, c, d], [far_x, far_z, (low, high)]


VMEM = pl.BlockSpec(memory_space=pltpu.VMEM)


def down_kernel(counts, x_ref, *refs):
    total = sum(counts)
    mine_ref, theirs_ref, square_ref = refs[total:]
    square = jnp.zeros((8, 128), jnp.float32)
    at, x = 0, x_ref[...]
    for i, count in enumerate(counts):
        step = x.shape[1] // count
        part = 0.0
        for j in range(count):
            block = refs[at][...]
            at += 1
            part += f32_dot(x[:, j * step : (j + 1) * step], block, ((1,), (0,)))
            wide = block.astype(jnp.float32)
            wide = jnp.sum((wide * wide).reshape(step // 8, 8, COLS), axis=0)
            square += wide[:, :128] + wide[:, 128:256] + wide[:, 256:]
        mine_ref[:, i * COLS : (i + 1) * COLS] = part[:64]
        theirs_ref[:, i * COLS : (i + 1) * COLS] = part[64:]
    square_ref[...] = square


def down_first(x, blocks):
    blocks = [b if isinstance(b, tuple) else (b,) for b in blocks]
    counts = [len(b) for b in blocks]
    flat = [piece for b in blocks for piece in b]
    n = len(blocks) * COLS
    return pl.pallas_call(
        lambda *refs: down_kernel(counts, *refs),
        out_shape=[jax.ShapeDtypeStruct((64, n), jnp.float32)] * 2 + [jax.ShapeDtypeStruct((8, 128), jnp.float32)],
        in_specs=[VMEM] * (1 + len(flat)),
        out_specs=[VMEM] * 3,
        compiler_params=pltpu.CompilerParams(vmem_limit_bytes=16 * 2**20),
        cost_estimate=pl.CostEstimate(
            flops=2 * x.size * n, bytes_accessed=2 * x.shape[1] * n, transcendentals=0
        ),
    )(x, *flat)


def core_sum(mine, theirs):
    return mine + other_core(theirs)


def sum_over_y(half, square=None):
    send = jnp.concatenate([h[16:].astype(jnp.bfloat16) for h in half], 1)
    n = send.shape[1]
    if square is not None:
        high = lax.reduce_precision(square, 8, 7)
        extra = jnp.concatenate([high, square - high]).astype(jnp.bfloat16)
        send = jnp.concatenate([send, jnp.tile(extra, (3, 1))], 1)
    got = lax.optimization_barrier(
        tuple(shift(send[16 * (d - 1) : 16 * d], "y", d) for d in (1, 3, 2))
    )
    total = jnp.concatenate([h[:16] for h in half], 1)
    for piece in got:
        total = total + piece[:, :n].astype(jnp.float32)
    if square is not None:
        for piece in got:
            square = square + piece[:8, n:].astype(jnp.float32) + piece[8:, n:].astype(jnp.float32)
    own = total.astype(jnp.bfloat16)
    up1, up3, up2 = (shift(own, "y", 4 - d) for d in (1, 3, 2))
    mine = [own, up1, up2, up3]
    return mine + [other_core(m) for m in mine], square


def apply_kernel(down, square_ref, *refs):
    t_refs, theta_refs, outs = refs[:8], refs[8 : 9 + BLOCKS], refs[9 + BLOCKS :]
    rows = theta_refs[0].shape[0]
    scale = ORDER / (4.0 * jnp.sum(square_ref[...]))

    def theta(i):
        if i < BLOCKS - 1:
            return theta_refs[i][...]
        return jnp.concatenate([theta_refs[i][...], theta_refs[i + 1][...]])

    total = jnp.zeros((128, rows), jnp.float32)
    for i in range(BLOCKS):
        t = jnp.concatenate([ref[:, i * COLS : (i + 1) * COLS] for ref in t_refs])
        total += f32_dot(t, theta(i), ((1,), (1,)))
    x = (total * scale).astype(jnp.bfloat16)
    if not down:
        outs[0][...] = x
        return
    for i in range(BLOCKS):
        part = f32_dot(x, theta(i), ((1,), (0,)))
        outs[0][:, i * COLS : (i + 1) * COLS] = part[:64]
        outs[1][:, i * COLS : (i + 1) * COLS] = part[64:]


def apply(square, t, blocks, down):
    n, rows = t[0].shape[1], blocks[0].shape[0]
    if down:
        out_shape = [jax.ShapeDtypeStruct((64, n), jnp.float32)] * 2
    else:
        out_shape = [jax.ShapeDtypeStruct((128, rows), jnp.bfloat16)]
    return pl.pallas_call(
        lambda *refs: apply_kernel(down, *refs),
        out_shape=out_shape,
        in_specs=[VMEM] * (1 + len(t) + len(blocks)),
        out_specs=[VMEM] * len(out_shape),
        compiler_params=pltpu.CompilerParams(vmem_limit_bytes=16 * 2**20),
        cost_estimate=pl.CostEstimate(
            flops=(4 if down else 2) * 128 * n * rows, bytes_accessed=2 * n * rows, transcendentals=0
        ),
    )(square, *t, *blocks)


def column_order(y, core):
    place = lax.broadcasted_iota(jnp.int32, (128, 128), 0)
    column = lax.broadcasted_iota(jnp.int32, (128, 128), 1)
    half = (place // 64 + core) % 2
    group = (place // 16 + y) % 4
    return (column == half * 64 + group * 16 + place % 16).astype(jnp.bfloat16)


def per_device(theta, basis):
    core, y = lax.axis_index("core"), lax.axis_index("y")
    order = column_order(y, core)
    x = f32_dot(order, basis, ((1,), (1,))).astype(jnp.bfloat16)

    blocks, half, square = [], [], 0.0
    for step in gather_plane(theta):
        mine, theirs, squares = down_first(x, step)
        half.append(core_sum(mine, theirs))
        square = square + squares
        blocks += step
    blocks = blocks[:-1] + list(blocks[-1])
    t, square = sum_over_y(half, square + other_core(square))
    t, _ = sum_over_y([core_sum(*apply(square, t, blocks, True))])
    (x,) = apply(square, t, blocks, False)
    subspace = f32_dot(x, order, ((0,), (0,))).astype(jnp.bfloat16)

    along_x = lax.all_gather(subspace, "x", axis=0)
    along_z = lax.all_to_all(jnp.broadcast_to(subspace[None], (4, *subspace.shape)), "z", 0, 0)
    part = jnp.einsum("brn,arm->bamn", along_z, along_x, preferred_element_type=jnp.float32)
    part = part.reshape(4, 4, 2, 64, 128).transpose(2, 0, 1, 3, 4).reshape(2, 16, 64, 128)
    keep = lax.dynamic_index_in_dim(part, core, 0, keepdims=False)
    half = keep + other_core(lax.dynamic_index_in_dim(part, 1 - core, 0, keepdims=False))
    got = lax.all_to_all(half, ("y", "x"), 0, 0).reshape(4, 4, 64, 128)
    sums = jnp.sum(got, axis=0).reshape(2, 2, 64, 128)
    keep = lax.dynamic_index_in_dim(sums, core, 0, keepdims=False)
    theirs = other_core(lax.dynamic_index_in_dim(sums, 1 - core, 0, keepdims=False))
    first_half = core == 0
    both = jnp.stack([jnp.where(first_half, keep, theirs), jnp.where(first_half, theirs, keep)])
    gram = both.transpose(0, 2, 1, 3).reshape(128, 256) / ORDER
    return subspace, gram


def solution(mesh):
    fine = Mesh(mesh.devices.reshape(4, 2, 4, 4), ALL)
    spec = P(("y", "core"), ("z", "x"))
    return jax.shard_map(
        per_device,
        mesh=fine,
        in_specs=(spec, spec),
        out_specs=(spec, P(("z", "x"), ("y", "core"))),
        check_vma=False,
    )
```

```python
import jax
import jax.numpy as jnp
from jax import lax
from jax.experimental import pallas as pl
from jax.experimental.pallas import tpu as pltpu
from jax.sharding import Mesh, PartitionSpec as P

ORDER = 6144
ALL = ("y", "core", "z", "x")
COLS = 384
BLOCKS = 16
KEPT = 5
SPLIT = 16


def shift(x, axis, by):
    return lax.ppermute(x, axis, [(i, (i + by) % 4) for i in range(4)])


def other_core(x):
    return lax.ppermute(x, "core", [(0, 1), (1, 0)])


def f32_dot(left, right, dims):
    return lax.dot_general(left, right, (dims, ((), ())), preferred_element_type=jnp.float32)


def after(x, *others):
    return lax.optimization_barrier((x, *others))[0]


def gather_and_apply(own, x):
    half = own.shape[0] // 2
    xp, xm, zp, zm = (shift(own, "x", 1), shift(own, "x", 3), shift(own, "z", 1), shift(own, "z", 3))
    first = down_first(x, [own, xp, xm, zp, zm], keep=True)
    pp, mm, pm, mp = (shift(zp, "x", 1), shift(zm, "x", 3), shift(xm, "z", 1), shift(xp, "z", 3))
    pp, mm, pm, mp = (after(block, first[2]) for block in (pp, mm, pm, mp))
    a, b, c, d = (shift(mp, "x", 1), shift(pm, "x", 3), shift(pp, "z", 1), shift(mm, "z", 3))
    second = down_first(x, [pp, mm, pm, mp])
    far_x, far_z, low, high = (shift(xp, "x", 1), shift(zp, "z", 1), shift(d[:half], "x", 3), shift(a[half:], "z", 3))
    third = down_first(x, [a, b, c, d])
    fourth = down_first(x, [far_x, far_z, (low, high)])
    blocks = [first[3], pp, mm, pm, mp, a, b, c, d, far_x, far_z, low, high]
    return blocks, [first[:3], second, third, fourth]


VMEM = pl.BlockSpec(memory_space=pltpu.VMEM)


def down_kernel(counts, keep, x_ref, *refs):
    total = sum(counts)
    mine_ref, theirs_ref, square_ref = refs[total : total + 3]
    square = jnp.zeros((8, 128), jnp.float32)
    at, x = 0, x_ref[...]
    for i, count in enumerate(counts):
        step = x.shape[1] // count
        part = 0.0
        for j in range(count):
            block = refs[at][...]
            if keep:
                refs[-1][at] = block
            at += 1
            part += f32_dot(x[:, j * step : (j + 1) * step], block, ((1,), (0,)))
            wide = block.astype(jnp.float32)
            wide = jnp.sum((wide * wide).reshape(step // 8, 8, COLS), axis=0)
            square += wide[:, :128] + wide[:, 128:256] + wide[:, 256:]
        mine_ref[:, i * COLS : (i + 1) * COLS] = part[:64]
        theirs_ref[:, i * COLS : (i + 1) * COLS] = part[64:]
    square_ref[...] = square


def down_first(x, blocks, keep=False):
    blocks = [b if isinstance(b, tuple) else (b,) for b in blocks]
    counts = [len(b) for b in blocks]
    flat = [piece for b in blocks for piece in b]
    n = len(blocks) * COLS
    out_shape = [jax.ShapeDtypeStruct((64, n), jnp.float32)] * 2 + [jax.ShapeDtypeStruct((8, 128), jnp.float32)]
    if keep:
        out_shape.append(jax.ShapeDtypeStruct((len(flat), *flat[0].shape), jnp.bfloat16))
    return pl.pallas_call(
        lambda *refs: down_kernel(counts, keep, *refs),
        out_shape=out_shape,
        in_specs=[VMEM] * (1 + len(flat)),
        out_specs=[VMEM] * len(out_shape),
        compiler_params=pltpu.CompilerParams(vmem_limit_bytes=12 * 2**20),
        cost_estimate=pl.CostEstimate(
            flops=2 * x.size * n, bytes_accessed=2 * x.shape[1] * n, transcendentals=0
        ),
    )(x, *flat)


def core_sum(mine, theirs):
    return mine + other_core(theirs)


def sum_over_y(half, square=None):
    send = jnp.concatenate([h[16:].astype(jnp.bfloat16) for h in half], 1)
    n = send.shape[1]
    if square is not None:
        high = lax.reduce_precision(square, 8, 7)
        extra = jnp.concatenate([high, square - high]).astype(jnp.bfloat16)
        send = jnp.concatenate([send, jnp.tile(extra, (3, 1))], 1)
    got = lax.optimization_barrier(
        tuple(shift(send[16 * (d - 1) : 16 * d], "y", d) for d in (1, 3, 2))
    )
    total = jnp.concatenate([h[:16] for h in half], 1)
    for piece in got:
        total = total + piece[:, :n].astype(jnp.float32)
    if square is not None:
        for piece in got:
            square = square + piece[:8, n:].astype(jnp.float32) + piece[8:, n:].astype(jnp.float32)
    own = total.astype(jnp.bfloat16)
    up1, up3, up2 = (shift(own, "y", 4 - d) for d in (1, 3, 2))
    mine = [own, up1, up2, up3]
    return mine + [other_core(m) for m in mine], square


def apply_kernel(down, widths, square_ref, *refs):
    pieces = 8 * len(widths)
    t_refs, (kept_ref, *theta_refs) = refs[:pieces], refs[pieces : pieces + BLOCKS - KEPT + 2]
    outs, t_ref = list(refs[pieces + BLOCKS - KEPT + 2 : -1]), refs[-1]
    rows = theta_refs[0].shape[0]
    at = 0
    for i, width in enumerate(widths):
        for j in range(8):
            t_ref[16 * j : 16 * j + 16, at : at + width] = t_refs[8 * i + j][...]
        at += width

    def theta(i):
        if i < KEPT:
            return kept_ref[i]
        if i < BLOCKS - 1:
            return theta_refs[i - KEPT][...]
        return jnp.concatenate([theta_refs[-2][...], theta_refs[-1][...]])

    if not down:
        order_ref, *outs = outs
    total = jnp.zeros((128, rows), jnp.float32)
    for i in range(BLOCKS):
        total += f32_dot(t_ref[:, i * COLS : (i + 1) * COLS], theta(i), ((1,), (1,)))
    scale = ORDER / (4.0 * jnp.sum(square_ref[...]))
    x = (total * scale).astype(jnp.bfloat16)
    if not down:
        subspace = f32_dot(x, order_ref[...], ((0,), (0,))).astype(jnp.bfloat16)
        outs[0][...] = subspace
        for i in range(4):
            outs[1][i] = subspace
        outs[2][...] = f32_dot(order_ref[...], x, ((0,), (0,))).astype(jnp.bfloat16)
        return
    for i in range(BLOCKS):
        part = f32_dot(x, theta(i), ((1,), (0,)))
        which, at = (0, i) if i < SPLIT else (1, i - SPLIT)
        outs[2 * which][:, at * COLS : (at + 1) * COLS] = part[:64]
        outs[2 * which + 1][:, at * COLS : (at + 1) * COLS] = part[64:]


def apply(square, t, blocks, order=None):
    widths = [piece.shape[1] for piece in t[::8]]
    n, rows = sum(widths), blocks[1].shape[0]
    down = order is None
    if down:
        out_shape = [jax.ShapeDtypeStruct((64, k * COLS), jnp.float32) for k in (SPLIT, BLOCKS - SPLIT) for _ in range(2) if k]
    else:
        out_shape = [jax.ShapeDtypeStruct(shape, jnp.bfloat16) for shape in ((rows, 128), (4, rows, 128), (128, rows))]
        blocks = [*blocks, order]
    return pl.pallas_call(
        lambda *refs: apply_kernel(down, widths, *refs),
        out_shape=out_shape,
        in_specs=[VMEM] * (1 + len(t) + len(blocks)),
        out_specs=[VMEM] * len(out_shape),
        scratch_shapes=[pltpu.VMEM((128, n), jnp.bfloat16)],
        compiler_params=pltpu.CompilerParams(vmem_limit_bytes=12 * 2**20),
        cost_estimate=pl.CostEstimate(
            flops=(4 if down else 2) * 128 * n * rows, bytes_accessed=2 * n * rows, transcendentals=0
        ),
    )(square, *t, *blocks)


def column_order(y, core):
    place = lax.broadcasted_iota(jnp.int32, (128, 128), 0)
    column = lax.broadcasted_iota(jnp.int32, (128, 128), 1)
    half = (place // 64 + core) % 2
    group = (place // 16 + y) % 4
    return (column == half * 64 + group * 16 + place % 16).astype(jnp.bfloat16)


def per_device(theta, basis):
    core, y = lax.axis_index("core"), lax.axis_index("y")
    order = column_order(y, core)
    x = f32_dot(order, basis, ((1,), (1,))).astype(jnp.bfloat16)

    blocks, steps = gather_and_apply(theta, x)
    half = [core_sum(mine, theirs) for mine, theirs, _ in steps]
    square = sum(squares for _, _, squares in steps)
    t, square = sum_over_y(half, square + other_core(square))
    t, _ = sum_over_y([core_sum(*apply(square, t, blocks))])
    subspace, copies, turned = apply(square, t, blocks, order)

    along_x = lax.all_gather(subspace, "x", axis=0)
    along_z = lax.all_to_all(copies, "z", 0, 0)
    part = jnp.einsum("brn,arm->bamn", along_z, along_x, preferred_element_type=jnp.float32)
    part = part.reshape(4, 4, 2, 64, 128).transpose(2, 0, 1, 3, 4).reshape(2, 16, 64, 128)
    keep = lax.dynamic_index_in_dim(part, core, 0, keepdims=False)
    half = keep + other_core(lax.dynamic_index_in_dim(part, 1 - core, 0, keepdims=False))
    got = lax.all_to_all(half, ("y", "x"), 0, 0).reshape(4, 4, 64, 128)
    sums = jnp.sum(got, axis=0).reshape(2, 2, 64, 128)
    keep = lax.dynamic_index_in_dim(sums, core, 0, keepdims=False)
    theirs = other_core(lax.dynamic_index_in_dim(sums, 1 - core, 0, keepdims=False))
    first_half = core == 0
    both = jnp.stack([jnp.where(first_half, keep, theirs), jnp.where(first_half, theirs, keep)])
    gram = both.transpose(0, 2, 1, 3).reshape(128, 256) / ORDER
    return subspace, gram


def solution(mesh):
    fine = Mesh(mesh.devices.reshape(4, 2, 4, 4), ALL)
    spec = P(("y", "core"), ("z", "x"))
    return jax.shard_map(
        per_device,
        mesh=fine,
        in_specs=(spec, spec),
        out_specs=(spec, P(("z", "x"), ("y", "core"))),
        check_vma=False,
    )
```

```python
import jax
import jax.numpy as jnp
from jax import lax
from jax.experimental import pallas as pl
from jax.experimental.pallas import tpu as pltpu
from jax.sharding import Mesh, PartitionSpec as P

ORDER = 6144
ALL = ("y", "core", "z", "x")
COLS = 384
BLOCKS = 16
KEPT = 5
SPLIT = 16


def shift(x, axis, by):
    return lax.ppermute(x, axis, [(i, (i + by) % 4) for i in range(4)])


def other_core(x):
    return lax.ppermute(x, "core", [(0, 1), (1, 0)])


def f32_dot(left, right, dims):
    return lax.dot_general(left, right, (dims, ((), ())), preferred_element_type=jnp.float32)


def after(x, *others):
    return lax.optimization_barrier((x, *others))[0]


def gather_and_apply(own, x):
    half = own.shape[0] // 2
    xp, xm, zp, zm = (shift(own, "x", 1), shift(own, "x", 3), shift(own, "z", 1), shift(own, "z", 3))
    first = down_first(x, [own, xp, xm, zp, zm], keep=True)
    pp, mm, pm, mp = (shift(zp, "x", 1), shift(zm, "x", 3), shift(xm, "z", 1), shift(xp, "z", 3))
    pp, mm, pm, mp = (after(block, first[2]) for block in (pp, mm, pm, mp))
    a, b, c, d = (shift(mp, "x", 1), shift(pm, "x", 3), shift(pp, "z", 1), shift(mm, "z", 3))
    second = down_first(x, [pp, mm, pm, mp])
    far_x, far_z, low, high = (shift(xp, "x", 1), shift(zp, "z", 1), shift(d[:half], "x", 3), shift(a[half:], "z", 3))
    third = down_first(x, [a, b, c, d])
    fourth = down_first(x, [far_x, far_z, (low, high)])
    blocks = [first[3], pp, mm, pm, mp, a, b, c, d, far_x, far_z, low, high]
    return blocks, [first[:3], second, third, fourth]


VMEM = pl.BlockSpec(memory_space=pltpu.VMEM)


def down_kernel(counts, keep, x_ref, *refs):
    total = sum(counts)
    mine_ref, theirs_ref, square_ref = refs[total : total + 3]
    square = jnp.zeros((8, 128), jnp.float32)
    at, x = 0, x_ref[...]
    for i, count in enumerate(counts):
        step = x.shape[1] // count
        part = 0.0
        for j in range(count):
            block = refs[at][...]
            if keep:
                refs[-1][at] = block
            at += 1
            part += f32_dot(x[:, j * step : (j + 1) * step], block, ((1,), (0,)))
            wide = block.astype(jnp.float32)
            wide = jnp.sum((wide * wide).reshape(step // 8, 8, COLS), axis=0)
            square += wide[:, :128] + wide[:, 128:256] + wide[:, 256:]
        mine_ref[:, i * COLS : (i + 1) * COLS] = part[:64]
        theirs_ref[:, i * COLS : (i + 1) * COLS] = part[64:]
    square_ref[...] = square


def down_first(x, blocks, keep=False):
    blocks = [b if isinstance(b, tuple) else (b,) for b in blocks]
    counts = [len(b) for b in blocks]
    flat = [piece for b in blocks for piece in b]
    n = len(blocks) * COLS
    out_shape = [jax.ShapeDtypeStruct((64, n), jnp.float32)] * 2 + [jax.ShapeDtypeStruct((8, 128), jnp.float32)]
    if keep:
        out_shape.append(jax.ShapeDtypeStruct((len(flat), *flat[0].shape), jnp.bfloat16))
    return pl.pallas_call(
        lambda *refs: down_kernel(counts, keep, *refs),
        out_shape=out_shape,
        in_specs=[VMEM] * (1 + len(flat)),
        out_specs=[VMEM] * len(out_shape),
        compiler_params=pltpu.CompilerParams(vmem_limit_bytes=12 * 2**20),
        cost_estimate=pl.CostEstimate(
            flops=2 * x.size * n, bytes_accessed=2 * x.shape[1] * n, transcendentals=0
        ),
    )(x, *flat)


def core_sum(mine, theirs):
    return mine + other_core(theirs)


def sum_over_y(half, square=None):
    send = jnp.concatenate([h[16:].astype(jnp.bfloat16) for h in half], 1)
    n = send.shape[1]
    if square is not None:
        high = lax.reduce_precision(square, 8, 7)
        extra = jnp.concatenate([high, square - high]).astype(jnp.bfloat16)
        send = jnp.concatenate([send, jnp.tile(extra, (3, 1))], 1)
    got = lax.optimization_barrier(
        tuple(shift(send[16 * (d - 1) : 16 * d], "y", d) for d in (1, 3, 2))
    )
    total = jnp.concatenate([h[:16] for h in half], 1)
    for piece in got:
        total = total + piece[:, :n].astype(jnp.float32)
    if square is not None:
        for piece in got:
            square = square + piece[:8, n:].astype(jnp.float32) + piece[8:, n:].astype(jnp.float32)
    own = total.astype(jnp.bfloat16)
    up1, up3, up2 = (shift(own, "y", 4 - d) for d in (1, 3, 2))
    mine = [own, up1, up2, up3]
    return mine + [other_core(m) for m in mine], square


def apply_kernel(down, widths, square_ref, *refs):
    pieces = 8 * len(widths)
    t_refs, (kept_ref, *theta_refs) = refs[:pieces], refs[pieces : pieces + BLOCKS - KEPT + 2]
    outs, t_ref = list(refs[pieces + BLOCKS - KEPT + 2 : -1]), refs[-1]
    rows = theta_refs[0].shape[0]
    at = 0
    for i, width in enumerate(widths):
        for j in range(8):
            t_ref[16 * j : 16 * j + 16, at : at + width] = t_refs[8 * i + j][...]
        at += width

    def theta(i):
        if i < KEPT:
            return kept_ref[i]
        if i < BLOCKS - 1:
            return theta_refs[i - KEPT][...]
        return jnp.concatenate([theta_refs[-2][...], theta_refs[-1][...]])

    if not down:
        order_ref, *outs = outs
    total = jnp.zeros((rows, 128), jnp.float32)
    for i in range(BLOCKS):
        total += f32_dot(theta(i), t_ref[:, i * COLS : (i + 1) * COLS], ((1,), (1,)))
    scale = ORDER / (4.0 * jnp.sum(square_ref[...]))
    x = (total * scale).astype(jnp.bfloat16)
    if not down:
        subspace = f32_dot(x, order_ref[...], ((1,), (0,))).astype(jnp.bfloat16)
        outs[0][...] = subspace
        for i in range(4):
            outs[1][i] = subspace
        return
    x = x.T
    for i in range(BLOCKS):
        part = f32_dot(x, theta(i), ((1,), (0,)))
        which, at = (0, i) if i < SPLIT else (1, i - SPLIT)
        outs[2 * which][:, at * COLS : (at + 1) * COLS] = part[:64]
        outs[2 * which + 1][:, at * COLS : (at + 1) * COLS] = part[64:]


def apply(square, t, blocks, order=None):
    widths = [piece.shape[1] for piece in t[::8]]
    n, rows = sum(widths), blocks[1].shape[0]
    down = order is None
    if down:
        out_shape = [jax.ShapeDtypeStruct((64, k * COLS), jnp.float32) for k in (SPLIT, BLOCKS - SPLIT) for _ in range(2) if k]
    else:
        out_shape = [jax.ShapeDtypeStruct(shape, jnp.bfloat16) for shape in ((rows, 128), (4, rows, 128))]
        blocks = [*blocks, order]
    return pl.pallas_call(
        lambda *refs: apply_kernel(down, widths, *refs),
        out_shape=out_shape,
        in_specs=[VMEM] * (1 + len(t) + len(blocks)),
        out_specs=[VMEM] * len(out_shape),
        scratch_shapes=[pltpu.VMEM((128, n), jnp.bfloat16)],
        compiler_params=pltpu.CompilerParams(vmem_limit_bytes=12 * 2**20),
        cost_estimate=pl.CostEstimate(
            flops=(4 if down else 2) * 128 * n * rows, bytes_accessed=2 * n * rows, transcendentals=0
        ),
    )(square, *t, *blocks)


def column_order(y, core):
    place = lax.broadcasted_iota(jnp.int32, (128, 128), 0)
    column = lax.broadcasted_iota(jnp.int32, (128, 128), 1)
    half = (place // 64 + core) % 2
    group = (place // 16 + y) % 4
    return (column == half * 64 + group * 16 + place % 16).astype(jnp.bfloat16)


def per_device(theta, basis):
    core, y = lax.axis_index("core"), lax.axis_index("y")
    order = column_order(y, core)
    x = f32_dot(order, basis, ((1,), (1,))).astype(jnp.bfloat16)

    blocks, steps = gather_and_apply(theta, x)
    half = [core_sum(mine, theirs) for mine, theirs, _ in steps]
    square = sum(squares for _, _, squares in steps)
    t, square = sum_over_y(half, square + other_core(square))
    t, _ = sum_over_y([core_sum(*apply(square, t, blocks))])
    subspace, copies = apply(square, t, blocks, order)

    along_x = lax.all_gather(subspace, "x", axis=0)
    along_z = lax.all_to_all(copies, "z", 0, 0)
    part = jnp.einsum("brn,arm->bamn", along_z, along_x, preferred_element_type=jnp.float32)
    part = part.reshape(4, 4, 2, 64, 128).transpose(2, 0, 1, 3, 4).reshape(2, 16, 64, 128)
    keep = lax.dynamic_index_in_dim(part, core, 0, keepdims=False)
    half = keep + other_core(lax.dynamic_index_in_dim(part, 1 - core, 0, keepdims=False))
    got = lax.all_to_all(half.astype(jnp.bfloat16), ("y", "x"), 0, 0).astype(jnp.float32).reshape(4, 4, 64, 128)
    sums = jnp.sum(got, axis=0).reshape(2, 2, 64, 128)
    keep = lax.dynamic_index_in_dim(sums, core, 0, keepdims=False)
    theirs = other_core(lax.dynamic_index_in_dim(sums, 1 - core, 0, keepdims=False))
    first_half = core == 0
    both = jnp.stack([jnp.where(first_half, keep, theirs), jnp.where(first_half, theirs, keep)])
    gram = both.transpose(0, 2, 1, 3).reshape(128, 256) / ORDER
    return subspace, gram


def solution(mesh):
    fine = Mesh(mesh.devices.reshape(4, 2, 4, 4), ALL)
    spec = P(("y", "core"), ("z", "x"))
    return jax.shard_map(
        per_device,
        mesh=fine,
        in_specs=(spec, spec),
        out_specs=(spec, P(("z", "x"), ("y", "core"))),
        check_vma=False,
    )
```

```python
import jax
import jax.numpy as jnp
from jax import lax
from jax.experimental import pallas as pl
from jax.experimental.pallas import tpu as pltpu
from jax.sharding import Mesh, PartitionSpec as P

ORDER = 6144
ALL = ("y", "core", "z", "x")
COLS = 384
BLOCKS = 16
KEPT = 5
SPLIT = 16


def shift(x, axis, by):
    return lax.ppermute(x, axis, [(i, (i + by) % 4) for i in range(4)])


def other_core(x):
    return lax.ppermute(x, "core", [(0, 1), (1, 0)])


def f32_dot(left, right, dims):
    return lax.dot_general(left, right, (dims, ((), ())), preferred_element_type=jnp.float32)


def after(x, *others):
    return lax.optimization_barrier((x, *others))[0]


def gather_and_apply(own, x):
    half = own.shape[0] // 2
    xp, xm, zp, zm = (shift(own, "x", 1), shift(own, "x", 3), shift(own, "z", 1), shift(own, "z", 3))
    first = down_first(x, [own, xp, xm, zp, zm], keep=True)
    pp, mm, pm, mp = (shift(zp, "x", 1), shift(zm, "x", 3), shift(xm, "z", 1), shift(xp, "z", 3))
    pp, mm, pm, mp = (after(block, first[2]) for block in (pp, mm, pm, mp))
    a, b, c, d = (shift(mp, "x", 1), shift(pm, "x", 3), shift(pp, "z", 1), shift(mm, "z", 3))
    second = down_first(x, [pp, mm, pm, mp])
    low, high = shift(d[:half], "x", 3), shift(a[half:], "z", 3)
    far_x, far_z = shift(after(xp, a), "x", 1), shift(after(zp, a), "z", 1)
    third = down_first(x, [a, b, c, d])
    early = reduce_y([core_sum(*step[:2]) for step in (first, second, third)])
    fourth = down_first(x, [far_x, far_z, (low, high)])
    blocks = [first[3], pp, mm, pm, mp, a, b, c, d, far_x, far_z, low, high]
    return blocks, early, fourth, first[2] + second[2] + third[2] + fourth[2]


VMEM = pl.BlockSpec(memory_space=pltpu.VMEM)


def down_kernel(counts, keep, x_ref, *refs):
    total = sum(counts)
    mine_ref, theirs_ref, square_ref = refs[total : total + 3]
    square = jnp.zeros((8, 128), jnp.float32)
    at, x = 0, x_ref[...]
    for i, count in enumerate(counts):
        step = x.shape[1] // count
        part = 0.0
        for j in range(count):
            block = refs[at][...]
            if keep:
                refs[-1][at] = block
            at += 1
            part += f32_dot(x[:, j * step : (j + 1) * step], block, ((1,), (0,)))
            wide = block.astype(jnp.float32)
            wide = jnp.sum((wide * wide).reshape(step // 8, 8, COLS), axis=0)
            square += wide[:, :128] + wide[:, 128:256] + wide[:, 256:]
        mine_ref[:, i * COLS : (i + 1) * COLS] = part[:64]
        theirs_ref[:, i * COLS : (i + 1) * COLS] = part[64:]
    square_ref[...] = square


def down_first(x, blocks, keep=False):
    blocks = [b if isinstance(b, tuple) else (b,) for b in blocks]
    counts = [len(b) for b in blocks]
    flat = [piece for b in blocks for piece in b]
    n = len(blocks) * COLS
    out_shape = [jax.ShapeDtypeStruct((64, n), jnp.float32)] * 2 + [jax.ShapeDtypeStruct((8, 128), jnp.float32)]
    if keep:
        out_shape.append(jax.ShapeDtypeStruct((len(flat), *flat[0].shape), jnp.bfloat16))
    return pl.pallas_call(
        lambda *refs: down_kernel(counts, keep, *refs),
        out_shape=out_shape,
        in_specs=[VMEM] * (1 + len(flat)),
        out_specs=[VMEM] * len(out_shape),
        compiler_params=pltpu.CompilerParams(vmem_limit_bytes=12 * 2**20),
        cost_estimate=pl.CostEstimate(
            flops=2 * x.size * n, bytes_accessed=2 * x.shape[1] * n, transcendentals=0
        ),
    )(x, *flat)


def core_sum(mine, theirs):
    return mine + other_core(theirs)


def sum_over_y(half):
    return gather_y(reduce_y(half))


def reduce_y(half):
    send = jnp.concatenate([h[16:].astype(jnp.bfloat16) for h in half], 1)
    sends = {d: send[16 * (d - 1) : 16 * d] for d in (1, 3, 2)}
    got = lax.optimization_barrier(tuple(shift(piece, "y", d) for d, piece in sends.items()))
    total = jnp.concatenate([h[:16] for h in half], 1)
    for piece in got:
        total = total + piece.astype(jnp.float32)
    return total.astype(jnp.bfloat16)


def gather_y(own):
    up1, up3, up2 = (shift(own, "y", 4 - d) for d in (1, 3, 2))
    mine = [own, up1, up2, up3]
    return mine + [other_core(m) for m in mine]


def sum_over_y_at_once(half, square):
    n = half.shape[1]
    high = lax.reduce_precision(square, 8, 7)
    extra = jnp.concatenate([high, square - high]).astype(jnp.bfloat16)
    send = jnp.concatenate([half.astype(jnp.bfloat16), jnp.tile(extra, (4, 1))], 1)
    got = lax.optimization_barrier(tuple(shift(send, "y", d) for d in (1, 3, 2)))
    total = half
    for d, piece in zip((1, 3, 2), got):
        turned = jnp.concatenate([piece[16 * d :, :n], piece[: 16 * d, :n]])
        total = total + turned.astype(jnp.float32)
        square = square + piece[:8, n:].astype(jnp.float32) + piece[8:16, n:].astype(jnp.float32)
    mine = total.astype(jnp.bfloat16)
    return [mine, other_core(mine)], square


def apply_kernel(down, count, square_ref, *refs):
    pieces = count
    t_refs, (kept_ref, *theta_refs) = refs[:pieces], refs[pieces : pieces + BLOCKS - KEPT + 2]
    outs, t_ref = list(refs[pieces + BLOCKS - KEPT + 2 : -1]), refs[-1]
    rows = theta_refs[0].shape[0]
    at, row = 0, 0
    for ref in t_refs:
        height, width = ref.shape
        t_ref[row : row + height, at : at + width] = ref[...]
        row += height
        if row == 128:
            at, row = at + width, 0

    def theta(i):
        if i < KEPT:
            return kept_ref[i]
        if i < BLOCKS - 1:
            return theta_refs[i - KEPT][...]
        return jnp.concatenate([theta_refs[-2][...], theta_refs[-1][...]])

    if not down:
        order_ref, *outs = outs
    total = jnp.zeros((rows, 128), jnp.float32)
    for i in range(BLOCKS):
        total += f32_dot(theta(i), t_ref[:, i * COLS : (i + 1) * COLS], ((1,), (1,)))
    scale = ORDER / (4.0 * jnp.sum(square_ref[...]))
    x = (total * scale).astype(jnp.bfloat16)
    if not down:
        subspace = f32_dot(x, order_ref[...], ((1,), (0,))).astype(jnp.bfloat16)
        outs[0][...] = subspace
        for i in range(4):
            outs[1][i] = subspace
        return
    x = x.T
    for i in range(BLOCKS):
        part = f32_dot(x, theta(i), ((1,), (0,)))
        which, at = (0, i) if i < SPLIT else (1, i - SPLIT)
        outs[2 * which][:, at * COLS : (at + 1) * COLS] = part[:64]
        outs[2 * which + 1][:, at * COLS : (at + 1) * COLS] = part[64:]


def apply(square, t, blocks, order=None):
    n, rows = sum(piece.size for piece in t) // 128, blocks[1].shape[0]
    down = order is None
    if down:
        out_shape = [jax.ShapeDtypeStruct((64, k * COLS), jnp.float32) for k in (SPLIT, BLOCKS - SPLIT) for _ in range(2) if k]
    else:
        out_shape = [jax.ShapeDtypeStruct(shape, jnp.bfloat16) for shape in ((rows, 128), (4, rows, 128))]
        blocks = [*blocks, order]
    return pl.pallas_call(
        lambda *refs: apply_kernel(down, len(t), *refs),
        out_shape=out_shape,
        in_specs=[VMEM] * (1 + len(t) + len(blocks)),
        out_specs=[VMEM] * len(out_shape),
        scratch_shapes=[pltpu.VMEM((128, n), jnp.bfloat16)],
        compiler_params=pltpu.CompilerParams(vmem_limit_bytes=12 * 2**20),
        cost_estimate=pl.CostEstimate(
            flops=(4 if down else 2) * 128 * n * rows, bytes_accessed=2 * n * rows, transcendentals=0
        ),
    )(square, *t, *blocks)


def column_order(y, core):
    place = lax.broadcasted_iota(jnp.int32, (128, 128), 0)
    column = lax.broadcasted_iota(jnp.int32, (128, 128), 1)
    half = (place // 64 + core) % 2
    group = (place // 16 + y) % 4
    return (column == half * 64 + group * 16 + place % 16).astype(jnp.bfloat16)


def per_device(theta, basis):
    core, y = lax.axis_index("core"), lax.axis_index("y")
    order = column_order(y, core)
    x = f32_dot(order, basis, ((1,), (1,))).astype(jnp.bfloat16)

    blocks, early, fourth, square = gather_and_apply(theta, x)
    late, square = sum_over_y_at_once(core_sum(*fourth[:2]), square + other_core(square))
    t = gather_y(early) + late
    t = sum_over_y([core_sum(*apply(square, t, blocks))])
    subspace, copies = apply(square, t, blocks, order)

    along_x = lax.all_gather(subspace, "x", axis=0)
    along_z = lax.all_to_all(copies, "z", 0, 0)
    part = jnp.einsum("brn,arm->bamn", along_z, along_x, preferred_element_type=jnp.float32)
    part = part.reshape(4, 4, 2, 64, 128).transpose(2, 0, 1, 3, 4).reshape(2, 16, 64, 128)
    keep = lax.dynamic_index_in_dim(part, core, 0, keepdims=False)
    half = keep + other_core(lax.dynamic_index_in_dim(part, 1 - core, 0, keepdims=False))
    got = lax.all_to_all(half.astype(jnp.bfloat16), ("y", "x"), 0, 0).astype(jnp.float32).reshape(4, 4, 64, 128)
    sums = jnp.sum(got, axis=0).reshape(2, 2, 64, 128)
    keep = lax.dynamic_index_in_dim(sums, core, 0, keepdims=False)
    theirs = other_core(lax.dynamic_index_in_dim(sums, 1 - core, 0, keepdims=False))
    first_half = core == 0
    both = jnp.stack([jnp.where(first_half, keep, theirs), jnp.where(first_half, theirs, keep)])
    gram = both.transpose(0, 2, 1, 3).reshape(128, 256) / ORDER
    return subspace, gram


def solution(mesh):
    fine = Mesh(mesh.devices.reshape(4, 2, 4, 4), ALL)
    spec = P(("y", "core"), ("z", "x"))
    return jax.shard_map(
        per_device,
        mesh=fine,
        in_specs=(spec, spec),
        out_specs=(spec, P(("z", "x"), ("y", "core"))),
        check_vma=False,
    )
```

```python
import jax
import jax.numpy as jnp
from jax import lax
from jax.experimental import pallas as pl
from jax.experimental.pallas import tpu as pltpu
from jax.sharding import Mesh, PartitionSpec as P

ORDER = 6144
ALL = ("y", "core", "z", "x")
COLS = 384
BLOCKS = 16
KEPT = 5
SPLIT = 8


def shift(x, axis, by):
    return lax.ppermute(x, axis, [(i, (i + by) % 4) for i in range(4)])


def other_core(x):
    return lax.ppermute(x, "core", [(0, 1), (1, 0)])


def f32_dot(left, right, dims):
    return lax.dot_general(left, right, (dims, ((), ())), preferred_element_type=jnp.float32)


def after(x, *others):
    return lax.optimization_barrier((x, *others))[0]


def gather_and_apply(own, x):
    half = own.shape[0] // 2
    xp, xm, zp, zm = (shift(own, "x", 1), shift(own, "x", 3), shift(own, "z", 1), shift(own, "z", 3))
    first = down_first(x, [own, xp, xm, zp, zm], keep=True)
    pp, mm, pm, mp = (shift(zp, "x", 1), shift(zm, "x", 3), shift(xm, "z", 1), shift(xp, "z", 3))
    pp, mm, pm, mp = (after(block, first[2]) for block in (pp, mm, pm, mp))
    a, b, c, d = (shift(mp, "x", 1), shift(pm, "x", 3), shift(pp, "z", 1), shift(mm, "z", 3))
    second = down_first(x, [pp, mm, pm, mp])
    low, high = shift(d[:half], "x", 3), shift(a[half:], "z", 3)
    far_x, far_z = shift(after(xp, a), "x", 1), shift(after(zp, a), "z", 1)
    third = down_first(x, [a, b, c, d])
    early = reduce_y([core_sum(*step[:2]) for step in (first, second, third)])
    fourth = down_first(x, [far_x, far_z, (low, high)])
    blocks = [first[3], pp, mm, pm, mp, a, b, c, d, far_x, far_z, low, high]
    return blocks, early, fourth, first[2] + second[2] + third[2] + fourth[2]


VMEM = pl.BlockSpec(memory_space=pltpu.VMEM)


def down_kernel(counts, keep, x_ref, *refs):
    total = sum(counts)
    mine_ref, theirs_ref, square_ref = refs[total : total + 3]
    square = jnp.zeros((8, 128), jnp.float32)
    at, x = 0, x_ref[...]
    for i, count in enumerate(counts):
        step = x.shape[1] // count
        part = 0.0
        for j in range(count):
            block = refs[at][...]
            if keep:
                refs[-1][at] = block
            at += 1
            part += f32_dot(x[:, j * step : (j + 1) * step], block, ((1,), (0,)))
            wide = block.astype(jnp.float32)
            wide = jnp.sum((wide * wide).reshape(step // 8, 8, COLS), axis=0)
            square += wide[:, :128] + wide[:, 128:256] + wide[:, 256:]
        mine_ref[:, i * COLS : (i + 1) * COLS] = part[:64]
        theirs_ref[:, i * COLS : (i + 1) * COLS] = part[64:]
    square_ref[...] = square


def down_first(x, blocks, keep=False):
    blocks = [b if isinstance(b, tuple) else (b,) for b in blocks]
    counts = [len(b) for b in blocks]
    flat = [piece for b in blocks for piece in b]
    n = len(blocks) * COLS
    out_shape = [jax.ShapeDtypeStruct((64, n), jnp.float32)] * 2 + [jax.ShapeDtypeStruct((8, 128), jnp.float32)]
    if keep:
        out_shape.append(jax.ShapeDtypeStruct((len(flat), *flat[0].shape), jnp.bfloat16))
    return pl.pallas_call(
        lambda *refs: down_kernel(counts, keep, *refs),
        out_shape=out_shape,
        in_specs=[VMEM] * (1 + len(flat)),
        out_specs=[VMEM] * len(out_shape),
        compiler_params=pltpu.CompilerParams(vmem_limit_bytes=12 * 2**20),
        cost_estimate=pl.CostEstimate(
            flops=2 * x.size * n, bytes_accessed=2 * x.shape[1] * n, transcendentals=0
        ),
    )(x, *flat)


def core_sum(mine, theirs):
    return mine + other_core(theirs)


def sum_over_y(half):
    return gather_y(reduce_y(half))


def reduce_y(half):
    send = jnp.concatenate([h[16:].astype(jnp.bfloat16) for h in half], 1)
    sends = {d: send[16 * (d - 1) : 16 * d] for d in (1, 3, 2)}
    got = lax.optimization_barrier(tuple(shift(piece, "y", d) for d, piece in sends.items()))
    total = jnp.concatenate([h[:16] for h in half], 1)
    for piece in got:
        total = total + piece.astype(jnp.float32)
    return total.astype(jnp.bfloat16)


def gather_y(own):
    up1, up3, up2 = (shift(own, "y", 4 - d) for d in (1, 3, 2))
    mine = [own, up1, up2, up3]
    return mine + [other_core(m) for m in mine]


def sum_over_y_at_once(half, square):
    n = half.shape[1]
    high = lax.reduce_precision(square, 8, 7)
    extra = jnp.concatenate([high, square - high]).astype(jnp.bfloat16)
    send = jnp.concatenate([half.astype(jnp.bfloat16), jnp.tile(extra, (4, 1))], 1)
    got = lax.optimization_barrier(tuple(shift(send, "y", d) for d in (1, 3, 2)))
    total = half
    for d, piece in zip((1, 3, 2), got):
        turned = jnp.concatenate([piece[16 * d :, :n], piece[: 16 * d, :n]])
        total = total + turned.astype(jnp.float32)
        square = square + piece[:8, n:].astype(jnp.float32) + piece[8:16, n:].astype(jnp.float32)
    mine = total.astype(jnp.bfloat16)
    return [mine, other_core(mine)], square


def apply_kernel(down, count, square_ref, *refs):
    pieces = count
    t_refs, (kept_ref, *theta_refs) = refs[:pieces], refs[pieces : pieces + BLOCKS - KEPT + 2]
    outs, t_ref = list(refs[pieces + BLOCKS - KEPT + 2 : -1]), refs[-1]
    rows = theta_refs[0].shape[0]
    at, row = 0, 0
    for ref in t_refs:
        height, width = ref.shape
        t_ref[row : row + height, at : at + width] = ref[...]
        row += height
        if row == 128:
            at, row = at + width, 0

    def theta(i):
        if i < KEPT:
            return kept_ref[i]
        if i < BLOCKS - 1:
            return theta_refs[i - KEPT][...]
        return jnp.concatenate([theta_refs[-2][...], theta_refs[-1][...]])

    if not down:
        order_ref, *outs = outs
    total = jnp.zeros((rows, 128), jnp.float32)
    for i in range(BLOCKS):
        total += f32_dot(theta(i), t_ref[:, i * COLS : (i + 1) * COLS], ((1,), (1,)))
    scale = ORDER / (4.0 * jnp.sum(square_ref[...]))
    x = (total * scale).astype(jnp.bfloat16)
    if not down:
        subspace = f32_dot(x, order_ref[...], ((1,), (0,))).astype(jnp.bfloat16)
        outs[0][...] = subspace
        for i in range(4):
            outs[1][i] = subspace
        return
    x = x.T
    for i in range(BLOCKS):
        part = f32_dot(x, theta(i), ((1,), (0,)))
        which, at = (0, i) if i < SPLIT else (1, i - SPLIT)
        outs[2 * which][:, at * COLS : (at + 1) * COLS] = part[:64]
        outs[2 * which + 1][:, at * COLS : (at + 1) * COLS] = part[64:]


def apply(square, t, blocks, order=None):
    n, rows = sum(piece.size for piece in t) // 128, blocks[1].shape[0]
    down = order is None
    if down:
        out_shape = [jax.ShapeDtypeStruct((64, k * COLS), jnp.float32) for k in (SPLIT, BLOCKS - SPLIT) for _ in range(2) if k]
    else:
        out_shape = [jax.ShapeDtypeStruct(shape, jnp.bfloat16) for shape in ((rows, 128), (4, rows, 128))]
        blocks = [*blocks, order]
    return pl.pallas_call(
        lambda *refs: apply_kernel(down, len(t), *refs),
        out_shape=out_shape,
        in_specs=[VMEM] * (1 + len(t) + len(blocks)),
        out_specs=[VMEM] * len(out_shape),
        scratch_shapes=[pltpu.VMEM((128, n), jnp.bfloat16)],
        compiler_params=pltpu.CompilerParams(vmem_limit_bytes=12 * 2**20),
        cost_estimate=pl.CostEstimate(
            flops=(4 if down else 2) * 128 * n * rows, bytes_accessed=2 * n * rows, transcendentals=0
        ),
    )(square, *t, *blocks)


def column_order(y, core):
    place = lax.broadcasted_iota(jnp.int32, (128, 128), 0)
    column = lax.broadcasted_iota(jnp.int32, (128, 128), 1)
    half = (place // 64 + core) % 2
    group = (place // 16 + y) % 4
    return (column == half * 64 + group * 16 + place % 16).astype(jnp.bfloat16)


def per_device(theta, basis):
    core, y = lax.axis_index("core"), lax.axis_index("y")
    order = column_order(y, core)
    x = f32_dot(order, basis, ((1,), (1,))).astype(jnp.bfloat16)

    blocks, early, fourth, square = gather_and_apply(theta, x)
    late, square = sum_over_y_at_once(core_sum(*fourth[:2]), square + other_core(square))
    t = gather_y(early) + late
    parts = apply(square, t, blocks)
    t = sum_over_y([core_sum(*parts[:2])]) + sum_over_y([core_sum(*parts[2:])])
    subspace, copies = apply(square, t, blocks, order)

    along_x = lax.all_gather(subspace, "x", axis=0)
    along_z = lax.all_to_all(copies, "z", 0, 0)
    part = jnp.einsum("brn,arm->bamn", along_z, along_x, preferred_element_type=jnp.float32)
    part = part.reshape(4, 4, 2, 64, 128).transpose(2, 0, 1, 3, 4).reshape(2, 16, 64, 128)
    keep = lax.dynamic_index_in_dim(part, core, 0, keepdims=False)
    half = keep + other_core(lax.dynamic_index_in_dim(part, 1 - core, 0, keepdims=False))
    got = lax.all_to_all(half.astype(jnp.bfloat16), ("y", "x"), 0, 0).astype(jnp.float32).reshape(4, 4, 64, 128)
    sums = jnp.sum(got, axis=0).reshape(2, 2, 64, 128)
    keep = lax.dynamic_index_in_dim(sums, core, 0, keepdims=False)
    theirs = other_core(lax.dynamic_index_in_dim(sums, 1 - core, 0, keepdims=False))
    first_half = core == 0
    both = jnp.stack([jnp.where(first_half, keep, theirs), jnp.where(first_half, theirs, keep)])
    gram = both.transpose(0, 2, 1, 3).reshape(128, 256) / ORDER
    return subspace, gram


def solution(mesh):
    fine = Mesh(mesh.devices.reshape(4, 2, 4, 4), ALL)
    spec = P(("y", "core"), ("z", "x"))
    return jax.shard_map(
        per_device,
        mesh=fine,
        in_specs=(spec, spec),
        out_specs=(spec, P(("z", "x"), ("y", "core"))),
        check_vma=False,
    )
```

```python
import jax
import jax.numpy as jnp
from jax import lax
from jax.experimental import pallas as pl
from jax.experimental.pallas import tpu as pltpu
from jax.sharding import Mesh, PartitionSpec as P

ORDER = 6144
ALL = ("y", "core", "z", "x")
COLS = 384
BLOCKS = 16
KEPT = 5
SPLIT = 8


def shift(x, axis, by):
    return lax.ppermute(x, axis, [(i, (i + by) % 4) for i in range(4)])


def other_core(x):
    return lax.ppermute(x, "core", [(0, 1), (1, 0)])


def f32_dot(left, right, dims):
    return lax.dot_general(left, right, (dims, ((), ())), preferred_element_type=jnp.float32)


def after(x, *others):
    return lax.optimization_barrier((x, *others))[0]


def gather_and_apply(own, x):
    half = own.shape[0] // 2
    xp, xm, zp, zm = (shift(own, "x", 1), shift(own, "x", 3), shift(own, "z", 1), shift(own, "z", 3))
    first = down_first(x, [own, xp, xm, zp, zm], keep=True)
    pp, mm, pm, mp = (shift(zp, "x", 1), shift(zm, "x", 3), shift(xm, "z", 1), shift(xp, "z", 3))
    pp, mm, pm, mp = (after(block, first[2]) for block in (pp, mm, pm, mp))
    a, b, c, d = (shift(mp, "x", 1), shift(pm, "x", 3), shift(pp, "z", 1), shift(mm, "z", 3))
    second = down_first(x, [pp, mm, pm, mp])
    low, high = shift(d[:half], "x", 3), shift(a[half:], "z", 3)
    far_x, far_z = shift(after(xp, mp), "x", 1), shift(after(zp, a), "z", 1)
    third = down_first(x, [a, b, c, d])
    early = reduce_y([core_sum(*step[:2]) for step in (first, second, third)])
    fourth = down_first(x, [far_x, far_z, (low, high)])
    blocks = [first[3], pp, mm, pm, mp, a, b, c, d, far_x, far_z, low, high]
    return blocks, early, fourth, first[2] + second[2] + third[2] + fourth[2]


VMEM = pl.BlockSpec(memory_space=pltpu.VMEM)


def down_kernel(counts, keep, x_ref, *refs):
    total = sum(counts)
    mine_ref, theirs_ref, square_ref = refs[total : total + 3]
    square = jnp.zeros((8, 128), jnp.float32)
    at, x = 0, x_ref[...]
    for i, count in enumerate(counts):
        step = x.shape[1] // count
        part = 0.0
        for j in range(count):
            block = refs[at][...]
            if keep:
                refs[-1][at] = block
            at += 1
            part += f32_dot(x[:, j * step : (j + 1) * step], block, ((1,), (0,)))
            wide = block.astype(jnp.float32)
            wide = jnp.sum((wide * wide).reshape(step // 8, 8, COLS), axis=0)
            square += wide[:, :128] + wide[:, 128:256] + wide[:, 256:]
        mine_ref[:, i * COLS : (i + 1) * COLS] = part[:64]
        theirs_ref[:, i * COLS : (i + 1) * COLS] = part[64:]
    square_ref[...] = square


def down_first(x, blocks, keep=False):
    blocks = [b if isinstance(b, tuple) else (b,) for b in blocks]
    counts = [len(b) for b in blocks]
    flat = [piece for b in blocks for piece in b]
    n = len(blocks) * COLS
    out_shape = [jax.ShapeDtypeStruct((64, n), jnp.float32)] * 2 + [jax.ShapeDtypeStruct((8, 128), jnp.float32)]
    if keep:
        out_shape.append(jax.ShapeDtypeStruct((len(flat), *flat[0].shape), jnp.bfloat16))
    return pl.pallas_call(
        lambda *refs: down_kernel(counts, keep, *refs),
        out_shape=out_shape,
        in_specs=[VMEM] * (1 + len(flat)),
        out_specs=[VMEM] * len(out_shape),
        compiler_params=pltpu.CompilerParams(vmem_limit_bytes=12 * 2**20),
        cost_estimate=pl.CostEstimate(
            flops=2 * x.size * n, bytes_accessed=2 * x.shape[1] * n, transcendentals=0
        ),
    )(x, *flat)


def core_sum(mine, theirs):
    return mine + other_core(theirs)


def sum_over_y(half):
    return gather_y(reduce_y(half))


def reduce_y(half):
    send = jnp.concatenate([h[16:].astype(jnp.bfloat16) for h in half], 1)
    sends = {d: send[16 * (d - 1) : 16 * d] for d in (1, 3, 2)}
    got = lax.optimization_barrier(tuple(shift(piece, "y", d) for d, piece in sorted(sends.items())))
    total = jnp.concatenate([h[:16] for h in half], 1)
    for piece in got:
        total = total + piece.astype(jnp.float32)
    return total.astype(jnp.bfloat16)


def gather_y(own):
    up2, up1, up3 = (shift(own, "y", 4 - d) for d in (2, 1, 3))
    mine = [own, up1, up2, up3]
    return mine + [other_core(m) for m in mine]


def sum_over_y_at_once(half, square):
    n = half.shape[1]
    high = lax.reduce_precision(square, 8, 7)
    extra = jnp.concatenate([high, square - high]).astype(jnp.bfloat16)
    send = jnp.concatenate([half.astype(jnp.bfloat16), jnp.tile(extra, (4, 1))], 1)
    got = lax.optimization_barrier(tuple(shift(send, "y", d) for d in (1, 3, 2)))
    total = half
    for d, piece in zip((1, 3, 2), got):
        turned = jnp.concatenate([piece[16 * d :, :n], piece[: 16 * d, :n]])
        total = total + turned.astype(jnp.float32)
        square = square + piece[:8, n:].astype(jnp.float32) + piece[8:16, n:].astype(jnp.float32)
    mine = total.astype(jnp.bfloat16)
    return [mine, other_core(mine)], square


def apply_kernel(down, count, square_ref, *refs):
    pieces = count
    t_refs, (kept_ref, *theta_refs) = refs[:pieces], refs[pieces : pieces + BLOCKS - KEPT + 2]
    outs, t_ref = list(refs[pieces + BLOCKS - KEPT + 2 : -1]), refs[-1]
    rows = theta_refs[0].shape[0]
    at, row = 0, 0
    for ref in t_refs:
        height, width = ref.shape
        t_ref[row : row + height, at : at + width] = ref[...]
        row += height
        if row == 128:
            at, row = at + width, 0

    def theta(i):
        if i < KEPT:
            return kept_ref[i]
        if i < BLOCKS - 1:
            return theta_refs[i - KEPT][...]
        return jnp.concatenate([theta_refs[-2][...], theta_refs[-1][...]])

    if not down:
        order_ref, *outs = outs
    total = jnp.zeros((rows, 128), jnp.float32)
    for i in range(BLOCKS):
        total += f32_dot(theta(i), t_ref[:, i * COLS : (i + 1) * COLS], ((1,), (1,)))
    scale = ORDER / (4.0 * jnp.sum(square_ref[...]))
    x = (total * scale).astype(jnp.bfloat16)
    if not down:
        subspace = f32_dot(x, order_ref[...], ((1,), (0,))).astype(jnp.bfloat16)
        outs[0][...] = subspace
        for i in range(4):
            outs[1][i] = subspace
        return
    x = x.T
    for i in range(BLOCKS):
        part = f32_dot(x, theta(i), ((1,), (0,)))
        which, at = (0, i) if i < SPLIT else (1, i - SPLIT)
        outs[2 * which][:, at * COLS : (at + 1) * COLS] = part[:64]
        outs[2 * which + 1][:, at * COLS : (at + 1) * COLS] = part[64:]


def apply(square, t, blocks, order=None):
    n, rows = sum(piece.size for piece in t) // 128, blocks[1].shape[0]
    down = order is None
    if down:
        out_shape = [jax.ShapeDtypeStruct((64, k * COLS), jnp.float32) for k in (SPLIT, BLOCKS - SPLIT) for _ in range(2) if k]
    else:
        out_shape = [jax.ShapeDtypeStruct(shape, jnp.bfloat16) for shape in ((rows, 128), (4, rows, 128))]
        blocks = [*blocks, order]
    return pl.pallas_call(
        lambda *refs: apply_kernel(down, len(t), *refs),
        out_shape=out_shape,
        in_specs=[VMEM] * (1 + len(t) + len(blocks)),
        out_specs=[VMEM] * len(out_shape),
        scratch_shapes=[pltpu.VMEM((128, n), jnp.bfloat16)],
        compiler_params=pltpu.CompilerParams(vmem_limit_bytes=12 * 2**20),
        cost_estimate=pl.CostEstimate(
            flops=(4 if down else 2) * 128 * n * rows, bytes_accessed=2 * n * rows, transcendentals=0
        ),
    )(square, *t, *blocks)


def column_order(y, core):
    place = lax.broadcasted_iota(jnp.int32, (128, 128), 0)
    column = lax.broadcasted_iota(jnp.int32, (128, 128), 1)
    half = (place // 64 + core) % 2
    group = (place // 16 + y) % 4
    return (column == half * 64 + group * 16 + place % 16).astype(jnp.bfloat16)


def per_device(theta, basis):
    core, y = lax.axis_index("core"), lax.axis_index("y")
    order = column_order(y, core)
    x = f32_dot(order, basis, ((1,), (1,))).astype(jnp.bfloat16)

    blocks, early, fourth, square = gather_and_apply(theta, x)
    late, square = sum_over_y_at_once(core_sum(*fourth[:2]), square + other_core(square))
    t = gather_y(early) + late
    parts = apply(square, t, blocks)
    t = sum_over_y([core_sum(*parts[:2])]) + sum_over_y([core_sum(*parts[2:])])
    subspace, copies = apply(square, t, blocks, order)

    along_x = lax.all_gather(subspace, "x", axis=0)
    along_z = lax.all_to_all(copies, "z", 0, 0)
    part = jnp.einsum("brn,arm->bamn", along_z, along_x, preferred_element_type=jnp.float32)
    part = part.reshape(4, 4, 2, 64, 128).transpose(2, 0, 1, 3, 4).reshape(2, 16, 64, 128)
    keep = lax.dynamic_index_in_dim(part, core, 0, keepdims=False)
    give = lax.dynamic_index_in_dim(part, 1 - core, 0, keepdims=False).astype(jnp.bfloat16)
    half = keep + other_core(give).astype(jnp.float32)
    got = lax.all_to_all(half.astype(jnp.bfloat16), ("y", "x"), 0, 0).astype(jnp.float32).reshape(4, 4, 64, 128)
    sums = jnp.sum(got, axis=0).reshape(2, 2, 64, 128)
    keep = lax.dynamic_index_in_dim(sums, core, 0, keepdims=False)
    theirs = other_core(lax.dynamic_index_in_dim(sums, 1 - core, 0, keepdims=False))
    first_half = core == 0
    both = jnp.stack([jnp.where(first_half, keep, theirs), jnp.where(first_half, theirs, keep)])
    gram = both.transpose(0, 2, 1, 3).reshape(128, 256) / ORDER
    return subspace, gram


def solution(mesh):
    fine = Mesh(mesh.devices.reshape(4, 2, 4, 4), ALL)
    spec = P(("y", "core"), ("z", "x"))
    return jax.shard_map(
        per_device,
        mesh=fine,
        in_specs=(spec, spec),
        out_specs=(spec, P(("z", "x"), ("y", "core"))),
        check_vma=False,
    )
```
